32 devices in a mesh: kvh: 2 (over x), ctx: 16 (over z, y, core).
Axes of the slice: x: 2, y: 2, z: 4, core: 2. Of those that a mesh axis runs over, the one named last changes fastest.
Arguments:
- queries: bfloat16 [512, 32, 128], P('ctx', 'kvh'), parts along dimension 1, may hold values from -6 to 6
- cache_keys: bfloat16 [16384, 256], P('ctx', 'kvh'), parts along dimension 1, may hold values from -6 to 6
- cache_values: bfloat16 [16384, 256], P('ctx', 'kvh'), parts along dimension 1, may hold values from -6 to 6
- span_offset: int32 [1], replicated, may hold values from 0 to 8191
- positions: int32 [512], replicated, may hold values from 0 to 8191
Outputs:
- attended: bfloat16 [512, 32, 128], P('ctx', 'kvh'), parts along dimension 1
The draws below stay inside these ranges and needn't reach their ends.
There are 2 independent parts, one for each index of `kvh`. The reference program is written for one: setup_inputs(seed, part) draws one part's arguments, and reference() takes and returns one part's arrays. A program takes and returns all parts, laid end to end along the dimension named above; an argument that names none is the same for every part. Nothing has to cross between parts.
All inputs are finite; a program needn't handle non-finite values.
Results may differ from the reference program's by a relative error of at most 0.0029.
Values may be sent and summed in bfloat16 or wider, within the bound.
A program may use at most 64 MiB of HBM per device.

```python
import jax
import jax.numpy as jnp
from jax import lax

HD = 128
QH = 16
TOK = 512
CTX_DEV = 1024
CONTEXT = 16384


def draw_queries(key, part):
    normal_part = jnp.clip(jax.random.normal(jax.random.fold_in(key, 13), (TOK, QH, HD), jnp.float32), -4.0, 4.0)
    return normal_part.astype(jnp.bfloat16)


def draw_cache_keys(key, part):
    normal_part = jnp.clip(jax.random.normal(jax.random.fold_in(key, 23), (CONTEXT, HD), jnp.float32), -3.0, 3.0)
    row_scale = jnp.exp(jax.random.uniform(jax.random.fold_in(key, 24), (CONTEXT, 1), jnp.float32, jnp.log(0.5), jnp.log(2.0)))
    normal_part = normal_part * row_scale
    return normal_part.astype(jnp.bfloat16)


def set_ends(result, rng, least, largest):
    longest = result.shape.index(max(result.shape))
    spots = []
    for shift in (0, 1):
        where = [jax.random.randint(jax.random.fold_in(rng, axis), (), 0, length) for axis, length in enumerate(result.shape)]
        where[longest] = (where[longest] + shift) % result.shape[longest]
        spots.append(tuple(where))
    return result.at[spots[0]].set(least).at[spots[1]].set(largest)


def block_levels(own_key, dims, shards, low, largest):
    def one(axis_at, shards_of):
        steps = jax.random.uniform(jax.random.fold_in(jax.random.fold_in(own_key, 6), axis_at), (shards_of,), jnp.float32, low / len(shards), largest / len(shards))
        return jnp.repeat(jnp.exp(steps), dims[axis_at] // shards_of).reshape((-1,) + (1,) * (len(dims) - axis_at - 1))

    factor_of = one(*shards[0])
    for cut in shards[1:]:
        factor_of = factor_of * one(*cut)
    return factor_of


def scatter_about(key, dims, scale, reach, split=(), held_as=jnp.bfloat16):
    loudness = block_levels(key, dims, split, -0.22, 0.18) if split else 1.0
    array = jax.random.normal(key, dims, jnp.float32) * scale * loudness
    return jnp.minimum(jnp.maximum(array, -reach), reach).astype(held_as)


def setup_inputs(seed: int = 0, part: int = 0) -> dict:
    splits = jax.random.split(jax.random.key(seed), 6)
    part_splits = jax.random.split(jax.random.fold_in(splits[5], part), 6)
    queries = draw_queries(jax.random.fold_in(jax.random.fold_in(splits[5], part), 71), part)
    cache_keys = draw_cache_keys(jax.random.fold_in(jax.random.fold_in(splits[5], part), 71), part)
    cache_values = scatter_about(part_splits[2], (CONTEXT, HD), 1.0, 6.0, ((0, 16),))
    span_offset = jax.random.randint(splits[3], (1,), 0, CONTEXT // 2).astype(jnp.int32)
    positions = set_ends(jax.random.randint(splits[4], (TOK,), 0, CONTEXT // 2), jax.random.fold_in(splits[4], 1), 0, (CONTEXT // 2) - 1).astype(jnp.int32)
    return {"queries": queries, "cache_keys": cache_keys, "cache_values": cache_values, "span_offset": span_offset, "positions": positions}


def reference(queries, cache_keys, cache_values, span_offset, positions):
    token_count, head_count, head_width = queries.shape
    row_count = token_count * head_count
    query_rows = queries.reshape(row_count, head_width)
    row_limit = jnp.repeat(span_offset[0] + positions, head_count)
    shard_total = cache_keys.shape[0] // CTX_DEV
    key_shards = cache_keys.reshape(shard_total, CTX_DEV, head_width)
    value_shards = cache_values.reshape(shard_total, CTX_DEV, head_width)
    score_scale = head_width ** -0.5

    def combine_shard(running, inputs):
        key_block, value_block, shard_index = inputs
        key_position = shard_index * CTX_DEV + jnp.arange(CTX_DEV, dtype=jnp.int32)
        scores = jnp.dot(query_rows, key_block.T, preferred_element_type=jnp.float32) * score_scale
        visible = key_position[None, :] <= row_limit[:, None]
        shard_max = jnp.max(jnp.where(visible, scores, -1e30), axis=1)
        weights = jnp.where(visible, jnp.exp(scores - shard_max[:, None]), 0.0).astype(jnp.bfloat16)
        shard_den = jnp.sum(weights.astype(jnp.float32), axis=1)
        shard_num = jnp.dot(weights, value_block, preferred_element_type=jnp.float32)
        run_top, run_num, run_den = running
        new_top = jnp.maximum(run_top, shard_max)
        keep = jnp.exp(run_top - new_top)
        fresh = jnp.exp(shard_max - new_top)
        return (new_top, run_num * keep[:, None] + shard_num * fresh[:, None], run_den * keep + shard_den * fresh), None

    start = (jnp.full((row_count,), -1e30, jnp.float32), jnp.zeros((row_count, head_width), jnp.float32), jnp.zeros((row_count,), jnp.float32))
    final_state, unused = lax.scan(combine_shard, start, (key_shards, value_shards, jnp.arange(shard_total, dtype=jnp.int32)))
    run_top, run_num, run_den = final_state
    return (run_num / run_den[:, None]).reshape(token_count, head_count, head_width).astype(jnp.bfloat16)
```

```python
import functools
import math

import jax
import jax.numpy as jnp
from jax import lax
from jax.experimental import pallas as pl
from jax.experimental.pallas import tpu as pltpu
from jax.sharding import PartitionSpec as P

FLOOR = -1e30
GROUP = 4
LANES = 128


def kernel(n, q_ref, k_ref, v_ref, off_ref, pos_ref, out_ref,
           qbuf, kbuf, vbuf, lim, num, den, top, psend, precv, lsend, lrecv,
           ks_sem, kr_sem, vs_sem, vr_sem, qs_sem, qr_sem, ps_sem, pr_sem, ls_sem, lr_sem):
    rows, width = q_ref.shape
    keys = k_ref.shape[0]
    tokens = pos_ref.shape[0] // (n * GROUP)
    heads = rows // tokens
    tile = min(128, rows)
    tiles = rows // tile
    c = width ** (-0.5) * math.log2(math.e)

    me = lax.axis_index("ctx")
    line = me // GROUP
    spot = me % GROUP
    up, core = spot // 2, spot % 2
    owners = (
        me,
        line * GROUP + up * 2 + (1 - core),
        line * GROUP + (1 - up) * 2 + core,
        line * GROUP + (1 - up) * 2 + (1 - core),
    )

    def ahead(k):
        return lax.rem(line + k, n) * GROUP + spot

    def behind(k):
        return lax.rem(line + n - k, n) * GROUP + spot

    def remote(src, dst, ssem, rsem, to):
        return pltpu.make_async_remote_copy(
            src_ref=src, dst_ref=dst, send_sem=ssem, recv_sem=rsem,
            device_id={"ctx": to}, device_id_type=pl.DeviceIdType.MESH)

    def q_copy(k):
        return remote(q_ref, qbuf.at[k], qs_sem.at[k], qr_sem.at[k], ahead(k))

    def p_copy(k):
        return remote(psend.at[k], precv.at[k], ps_sem.at[k], pr_sem.at[k], behind(k))

    def l_copy(k):
        return remote(lsend.at[k], lrecv.at[k], ls_sem.at[k], lr_sem.at[k], behind(k))

    k_copies = [
        remote(k_ref, kbuf.at[0], ks_sem.at[0], kr_sem.at[0], owners[1]),
        remote(k_ref, kbuf.at[1], ks_sem.at[1], kr_sem.at[1], owners[2]),
        remote(kbuf.at[1], kbuf.at[2], ks_sem.at[2], kr_sem.at[2], owners[1]),
    ]
    v_copies = [
        remote(v_ref, vbuf.at[0], vs_sem.at[0], vr_sem.at[0], owners[1]),
        remote(v_ref, vbuf.at[1], vs_sem.at[1], vr_sem.at[1], owners[2]),
        remote(vbuf.at[1], vbuf.at[2], vs_sem.at[2], vr_sem.at[2], owners[1]),
    ]

    barrier = pltpu.get_barrier_semaphore()
    for to in (owners[1], owners[2]):
        pl.semaphore_signal(barrier, inc=1, device_id={"ctx": to}, device_id_type=pl.DeviceIdType.MESH)

    @pl.loop(1, n)
    def _(k):
        pl.semaphore_signal(barrier, inc=1, device_id={"ctx": ahead(k)}, device_id_type=pl.DeviceIdType.MESH)

    @pl.loop(0, n)
    def _(k):
        first = behind(k) * tokens

        @pl.loop(0, tokens)
        def _(t):
            limit = off_ref[0] + pos_ref[first + t]
            lim[k, pl.ds(pl.multiple_of(t * heads, heads), heads), :] = jnp.full((heads, LANES), limit, jnp.int32)

    qbuf[0] = q_ref[...]
    pl.semaphore_wait(barrier, n + 1)

    k_copies[1].start()
    v_copies[1].start()
    k_copies[0].start()
    v_copies[0].start()

    @pl.loop(1, n)
    def _(k):
        q_copy(k).start()

    lane = lax.broadcasted_iota(jnp.int32, (1, LANES), 1)
    diagonal = (lax.broadcasted_iota(jnp.int32, (tile, LANES), 0)
                == lax.broadcasted_iota(jnp.int32, (tile, LANES), 1))
    ones = jnp.ones((keys, LANES), jnp.bfloat16)

    def block(slot, at, b):
        key_block = k_ref[...] if b == 0 else kbuf[b - 1]
        value_block = v_ref[...] if b == 0 else vbuf[b - 1]
        scores = lax.dot_general(qbuf[slot, at, :], key_block, (((1,), (1,)), ((), ())),
                                 preferred_element_type=jnp.float32)
        limit = lim[slot, at, :]
        base = owners[b] * keys
        parts = []
        for j in range(keys // LANES):
            seen = lane + (base + j * LANES) <= limit
            parts.append(jnp.where(seen, scores[:, j * LANES:(j + 1) * LANES], FLOOR))
        high = functools.reduce(jnp.maximum, parts)
        high = jnp.broadcast_to(jnp.max(high, axis=1, keepdims=True), (tile, LANES))
        weights = jnp.concatenate(
            [jnp.exp2((part - high) * c).astype(jnp.bfloat16) for part in parts], axis=1)
        both = jnp.dot(weights, jnp.concatenate([value_block, ones], axis=1),
                       preferred_element_type=jnp.float32)
        return both[:, :width], both[:, width:], high

    def merge(a, b):
        high = jnp.maximum(a[2], b[2])
        fa, fb = jnp.exp2((a[2] - high) * c), jnp.exp2((b[2] - high) * c)
        return a[0] * fa + b[0] * fb, a[1] * fa + b[1] * fb, high

    def spread(t):
        return pl.ds(pl.multiple_of(t * tile, tile), tile)

    def keep(slot, at, state):
        num[slot, at, :], den[slot, at, :], top[slot, at, :] = state

    def kept(slot, at):
        return num[slot, at, :], den[slot, at, :], top[slot, at, :]

    @pl.loop(0, tiles)
    def _(t):
        keep(0, spread(t), block(0, spread(t), 0))

    k_copies[0].wait_recv()
    v_copies[0].wait_recv()

    @pl.loop(0, tiles)
    def _(t):
        keep(0, spread(t), merge(kept(0, spread(t)), block(0, spread(t), 1)))

    @pl.loop(1, n)
    def _(k):
        q_copy(k).wait_recv()

        @pl.loop(0, tiles)
        def _(t):
            keep(k, spread(t), merge(block(k, spread(t), 0), block(k, spread(t), 1)))

    k_copies[1].wait_recv()
    k_copies[2].start()
    v_copies[1].wait_recv()
    v_copies[2].start()

    @pl.loop(0, n)
    def _(k):
        @pl.loop(0, tiles)
        def _(t):
            keep(k, spread(t), merge(kept(k, spread(t)), block(k, spread(t), 2)))

    k_copies[2].wait_recv()
    v_copies[2].wait_recv()

    @pl.loop(1, n)
    def _(k):
        @pl.loop(0, tiles)
        def _(t):
            at = spread(t)
            top_num, top_den, high = merge(kept(k, at), block(k, at, 3))
            psend[k, at, :] = (top_num / top_den).astype(jnp.bfloat16)
            size = high * c + jnp.log2(top_den)
            lsend[k, pl.ds(t, 1), :] = jnp.sum(jnp.where(diagonal, size, 0.0), axis=0, keepdims=True)

        p_copy(k).start()
        l_copy(k).start()

    @pl.loop(0, tiles)
    def _(t):
        at = spread(t)
        top_num, top_den, high = merge(kept(0, at), block(0, at, 3))
        num[0, at, :] = top_num / top_den
        top[0, at, :] = high * c + jnp.log2(top_den)

    @pl.loop(1, n)
    def _(k):
        p_copy(k).wait_recv()
        l_copy(k).wait_recv()

    @pl.loop(0, tiles)
    def _(t):
        at = spread(t)

        def size_of(k):
            line_of = jnp.broadcast_to(lrecv[k, pl.ds(t, 1), :], (tile, LANES))
            return jnp.broadcast_to(
                jnp.sum(jnp.where(diagonal, line_of, 0.0), axis=1, keepdims=True), (tile, LANES))

        def step(k, state):
            total, mass, high = state
            size = size_of(k)
            higher = jnp.maximum(high, size)
            old, new = jnp.exp2(high - higher), jnp.exp2(size - higher)
            return total * old + precv[k, at, :].astype(jnp.float32) * new, mass * old + new, higher

        state = (num[0, at, :], jnp.ones((tile, LANES), jnp.float32), top[0, at, :])
        if n <= 8:
            for k in range(1, n):
                state = step(k, state)
        else:
            state = lax.fori_loop(1, n, step, state)
        out_ref[at, :] = (state[0] / state[1]).astype(out_ref.dtype)

    for copy in (*k_copies, *v_copies):
        copy.wait_send()

    @pl.loop(1, n)
    def _(k):
        q_copy(k).wait_send()
        p_copy(k).wait_send()
        l_copy(k).wait_send()


def local(n, queries, cache_keys, cache_values, span_offset, positions):
    tokens, heads, width = queries.shape
    rows = tokens * heads
    keys = cache_keys.shape[0]
    tile = min(128, rows)
    marks = max(8, rows // tile)
    vmem = pl.BlockSpec(memory_space=pltpu.VMEM)
    smem = pl.BlockSpec(memory_space=pltpu.SMEM)
    dma = pltpu.SemaphoreType.DMA
    out = pl.pallas_call(
        functools.partial(kernel, n),
        out_shape=jax.ShapeDtypeStruct((rows, width), jnp.bfloat16),
        in_specs=[vmem, vmem, vmem, smem, smem],
        out_specs=vmem,
        scratch_shapes=[
            pltpu.VMEM((n, rows, width), jnp.bfloat16),
            pltpu.VMEM((3, keys, width), jnp.bfloat16),
            pltpu.VMEM((3, keys, width), jnp.bfloat16),
            pltpu.VMEM((n, rows, LANES), jnp.int32),
            pltpu.VMEM((n, rows, width), jnp.float32),
            pltpu.VMEM((n, rows, LANES), jnp.float32),
            pltpu.VMEM((n, rows, LANES), jnp.float32),
            pltpu.VMEM((n, rows, width), jnp.bfloat16),
            pltpu.VMEM((n, rows, width), jnp.bfloat16),
            pltpu.VMEM((n, marks, LANES), jnp.float32),
            pltpu.VMEM((n, marks, LANES), jnp.float32),
            dma((3,)), dma((3,)), dma((3,)), dma((3,)),
            dma((n,)), dma((n,)), dma((n,)), dma((n,)), dma((n,)), dma((n,)),
        ],
        compiler_params=pltpu.CompilerParams(
            collective_id=0, has_side_effects=True, vmem_limit_bytes=40 * 1024 * 1024),
    )(queries.reshape(rows, width), cache_keys, cache_values, span_offset, positions)
    return out.reshape(tokens, heads, width)


def solution(mesh):
    n = mesh.shape["ctx"] // GROUP
    in_specs = (P("ctx", "kvh", None), P("ctx", "kvh"), P("ctx", "kvh"), P(), P())
    return jax.shard_map(functools.partial(local, n), mesh=mesh, in_specs=in_specs,
                         out_specs=P("ctx", "kvh", None), check_vma=False)
```

```python
import functools
import math

import jax
import jax.numpy as jnp
from jax import lax
from jax.experimental import pallas as pl
from jax.experimental.pallas import tpu as pltpu
from jax.sharding import PartitionSpec as P

FLOOR = -1e30
GROUP = 4
LANES = 128


def kernel(n, q_ref, k_ref, v_ref, off_ref, pos_ref, out_ref,
           qbuf, kbuf, vbuf, lim, num, den, top, psend, precv, lsend, lrecv,
           own_sem, ks_sem, kr_sem, vs_sem, vr_sem, qs_sem, qr_sem, ps_sem, pr_sem, ls_sem, lr_sem):
    rows, width = q_ref.shape
    keys = k_ref.shape[0]
    tokens = pos_ref.shape[0] // (n * GROUP)
    heads = rows // tokens
    tile = min(128, rows)
    tiles = rows // tile
    unroll = min(4, tiles)
    c = width ** (-0.5) * math.log2(math.e)

    me = lax.axis_index("ctx")
    line = me // GROUP
    spot = me % GROUP
    up, core = spot // 2, spot % 2
    owners = (
        me,
        line * GROUP + up * 2 + (1 - core),
        line * GROUP + (1 - up) * 2 + core,
        line * GROUP + (1 - up) * 2 + (1 - core),
    )

    def ahead(k):
        return lax.rem(line + k, n) * GROUP + spot

    def behind(k):
        return lax.rem(line + n - k, n) * GROUP + spot

    def remote(src, dst, ssem, rsem, to):
        return pltpu.make_async_remote_copy(
            src_ref=src, dst_ref=dst, send_sem=ssem, recv_sem=rsem,
            device_id={"ctx": to}, device_id_type=pl.DeviceIdType.MESH)

    def q_copy(k):
        return remote(q_ref, qbuf.at[k], qs_sem.at[k], qr_sem.at[k], ahead(k))

    def p_copy(k):
        return remote(psend.at[k], precv.at[k], ps_sem.at[k], pr_sem.at[k], behind(k))

    def l_copy(k):
        return remote(lsend.at[k], lrecv.at[k], ls_sem.at[k], lr_sem.at[k], behind(k))

    k_copies = [
        remote(k_ref, kbuf.at[1], ks_sem.at[0], kr_sem.at[0], owners[1]),
        remote(k_ref, kbuf.at[2], ks_sem.at[1], kr_sem.at[1], owners[2]),
        remote(kbuf.at[2], kbuf.at[3], ks_sem.at[2], kr_sem.at[2], owners[1]),
    ]
    v_copies = [
        remote(v_ref, vbuf.at[1], vs_sem.at[0], vr_sem.at[0], owners[1]),
        remote(v_ref, vbuf.at[2], vs_sem.at[1], vr_sem.at[1], owners[2]),
        remote(vbuf.at[2], vbuf.at[3], vs_sem.at[2], vr_sem.at[2], owners[1]),
    ]

    own_copies = [
        pltpu.make_async_copy(q_ref, qbuf.at[0], own_sem.at[0]),
        pltpu.make_async_copy(k_ref, kbuf.at[0], own_sem.at[1]),
        pltpu.make_async_copy(v_ref, vbuf.at[0], own_sem.at[2]),
    ]
    for copy in own_copies:
        copy.start()

    barrier = pltpu.get_barrier_semaphore()
    for to in (owners[1], owners[2]):
        pl.semaphore_signal(barrier, inc=1, device_id={"ctx": to}, device_id_type=pl.DeviceIdType.MESH)

    @pl.loop(1, n)
    def _(k):
        pl.semaphore_signal(barrier, inc=1, device_id={"ctx": ahead(k)}, device_id_type=pl.DeviceIdType.MESH)

    pl.semaphore_wait(barrier, n + 1)

    k_copies[1].start()
    v_copies[1].start()
    k_copies[0].start()
    v_copies[0].start()

    @pl.loop(1, n)
    def _(k):
        q_copy(k).start()

    @pl.loop(0, n)
    def _(k):
        first = behind(k) * tokens

        @pl.loop(0, tokens)
        def _(t):
            limit = off_ref[0] + pos_ref[first + t]
            lim[k, pl.ds(pl.multiple_of(t * heads, heads), heads), :] = jnp.full((heads, LANES), limit, jnp.int32)

    for copy in own_copies:
        copy.wait()

    lane = lax.broadcasted_iota(jnp.int32, (1, LANES), 1)
    diagonal = (lax.broadcasted_iota(jnp.int32, (tile, LANES), 0)
                == lax.broadcasted_iota(jnp.int32, (tile, LANES), 1))
    ones = jnp.ones((keys, LANES), jnp.bfloat16)

    def block(slot, at, b):
        key_block = kbuf[b]
        value_block = vbuf[b]
        scores = lax.dot_general(qbuf[slot, at, :], key_block, (((1,), (1,)), ((), ())),
                                 preferred_element_type=jnp.float32)
        limit = lim[slot, at, :]
        base = owners[b] * keys
        parts = []
        for j in range(keys // LANES):
            seen = lane + (base + j * LANES) <= limit
            parts.append(jnp.where(seen, scores[:, j * LANES:(j + 1) * LANES], FLOOR))
        high = functools.reduce(jnp.maximum, parts)
        high = jnp.broadcast_to(jnp.max(high, axis=1, keepdims=True), (tile, LANES))
        weights = jnp.concatenate(
            [jnp.exp2((part - high) * c).astype(jnp.bfloat16) for part in parts], axis=1)
        both = jnp.dot(weights, jnp.concatenate([value_block, ones], axis=1),
                       preferred_element_type=jnp.float32)
        return both[:, :width], both[:, width:], high

    def merge(a, b):
        high = jnp.maximum(a[2], b[2])
        fa, fb = jnp.exp2((a[2] - high) * c), jnp.exp2((b[2] - high) * c)
        return a[0] * fa + b[0] * fb, a[1] * fa + b[1] * fb, high

    def spread(t):
        return pl.ds(pl.multiple_of(t * tile, tile), tile)

    def keep(slot, at, state):
        num[slot, at, :], den[slot, at, :], top[slot, at, :] = state

    def kept(slot, at):
        return num[slot, at, :], den[slot, at, :], top[slot, at, :]

    @pl.loop(0, tiles, unroll=unroll)
    def _(t):
        keep(0, spread(t), block(0, spread(t), 0))

    k_copies[0].wait_recv()
    v_copies[0].wait_recv()

    @pl.loop(0, tiles, unroll=unroll)
    def _(t):
        keep(0, spread(t), merge(kept(0, spread(t)), block(0, spread(t), 1)))

    @pl.loop(1, n)
    def _(k):
        q_copy(k).wait_recv()

        @pl.loop(0, tiles, unroll=unroll)
        def _(t):
            keep(k, spread(t), merge(block(k, spread(t), 0), block(k, spread(t), 1)))

    k_copies[1].wait_recv()
    k_copies[2].start()
    v_copies[1].wait_recv()
    v_copies[2].start()

    @pl.loop(0, tiles, unroll=unroll)
    def _(t):
        keep(0, spread(t), merge(kept(0, spread(t)), block(0, spread(t), 2)))

    k_copies[2].wait_recv()
    v_copies[2].wait_recv()

    @pl.loop(1, n)
    def _(k):
        @pl.loop(0, tiles, unroll=unroll)
        def _(t):
            at = spread(t)
            top_num, top_den, high = merge(kept(k, at), merge(block(k, at, 2), block(k, at, 3)))
            psend[k, at, :] = (top_num / top_den).astype(jnp.bfloat16)
            size = high * c + jnp.log2(top_den)
            lsend[k, pl.ds(t, 1), :] = jnp.sum(jnp.where(diagonal, size, 0.0), axis=0, keepdims=True)

        p_copy(k).start()
        l_copy(k).start()

    @pl.loop(0, tiles, unroll=unroll)
    def _(t):
        at = spread(t)
        top_num, top_den, high = merge(kept(0, at), block(0, at, 3))
        num[0, at, :] = top_num / top_den
        top[0, at, :] = high * c + jnp.log2(top_den)

    @pl.loop(1, n)
    def _(k):
        p_copy(k).wait_recv()
        l_copy(k).wait_recv()

    @pl.loop(0, tiles, unroll=unroll)
    def _(t):
        at = spread(t)

        def size_of(k):
            line_of = jnp.broadcast_to(lrecv[k, pl.ds(t, 1), :], (tile, LANES))
            return jnp.broadcast_to(
                jnp.sum(jnp.where(diagonal, line_of, 0.0), axis=1, keepdims=True), (tile, LANES))

        def step(k, state):
            total, mass, high = state
            size = size_of(k)
            higher = jnp.maximum(high, size)
            old, new = jnp.exp2(high - higher), jnp.exp2(size - higher)
            return total * old + precv[k, at, :].astype(jnp.float32) * new, mass * old + new, higher

        state = (num[0, at, :], jnp.ones((tile, LANES), jnp.float32), top[0, at, :])
        if n <= 8:
            for k in range(1, n):
                state = step(k, state)
        else:
            state = lax.fori_loop(1, n, step, state)
        out_ref[at, :] = (state[0] / state[1]).astype(out_ref.dtype)

    for copy in (*k_copies, *v_copies):
        copy.wait_send()

    @pl.loop(1, n)
    def _(k):
        q_copy(k).wait_send()
        p_copy(k).wait_send()
        l_copy(k).wait_send()


def local(n, queries, cache_keys, cache_values, span_offset, positions):
    tokens, heads, width = queries.shape
    rows = tokens * heads
    keys = cache_keys.shape[0]
    tile = min(128, rows)
    marks = max(8, rows // tile)
    vmem = pl.BlockSpec(memory_space=pltpu.VMEM)
    hbm = pl.BlockSpec(memory_space=pltpu.HBM)
    smem = pl.BlockSpec(memory_space=pltpu.SMEM)
    dma = pltpu.SemaphoreType.DMA
    out = pl.pallas_call(
        functools.partial(kernel, n),
        out_shape=jax.ShapeDtypeStruct((rows, width), jnp.bfloat16),
        in_specs=[hbm, hbm, hbm, smem, smem],
        out_specs=vmem,
        scratch_shapes=[
            pltpu.VMEM((n, rows, width), jnp.bfloat16),
            pltpu.VMEM((4, keys, width), jnp.bfloat16),
            pltpu.VMEM((4, keys, width), jnp.bfloat16),
            pltpu.VMEM((n, rows, LANES), jnp.int32),
            pltpu.VMEM((n, rows, width), jnp.float32),
            pltpu.VMEM((n, rows, LANES), jnp.float32),
            pltpu.VMEM((n, rows, LANES), jnp.float32),
            pltpu.VMEM((n, rows, width), jnp.bfloat16),
            pltpu.VMEM((n, rows, width), jnp.bfloat16),
            pltpu.VMEM((n, marks, LANES), jnp.float32),
            pltpu.VMEM((n, marks, LANES), jnp.float32),
            dma((3,)), dma((3,)), dma((3,)), dma((3,)), dma((3,)),
            dma((n,)), dma((n,)), dma((n,)), dma((n,)), dma((n,)), dma((n,)),
        ],
        compiler_params=pltpu.CompilerParams(
            collective_id=0, has_side_effects=True, vmem_limit_bytes=56 * 1024 * 1024),
    )(queries.reshape(rows, width), cache_keys, cache_values, span_offset, positions)
    return out.reshape(tokens, heads, width)


def solution(mesh):
    n = mesh.shape["ctx"] // GROUP
    in_specs = (P("ctx", "kvh", None), P("ctx", "kvh"), P("ctx", "kvh"), P(), P())
    return jax.shard_map(functools.partial(local, n), mesh=mesh, in_specs=in_specs,
                         out_specs=P("ctx", "kvh", None), check_vma=False)
```
